32 devices in a mesh: mol: 2 (over y), vir: 16 (over z, x, core), occ: 1.
Axes of the slice: x: 2, y: 2, z: 4, core: 2. Of those that a mesh axis runs over, the one named last changes fastest.
Arguments:
- amplitudes: float32 [384, 16384], P(('mol', 'occ'), 'vir'), parts along dimension 0, may hold values from -6 to 6
- ladder_ints: float32 [49152, 1536], P(('mol', 'vir')), parts along dimension 0, may hold values from -0.15625 to 0.15625
- hole_ints: float32 [384, 192], P('mol', 'occ'), parts along dimension 0, may hold values from -0.4375 to 0.4375
- sector_sizes: int32 [16], replicated, may hold values from 1 to 12, 128 in all
- device_perm: int32 [16], replicated, may hold values from 0 to 15, each once
- block_shift: int32 [16], replicated, may hold values from 0 to 7
Outputs:
- residual: float32 [384, 16384], P(('mol', 'occ'), 'vir'), parts along dimension 0
The draws below stay inside these ranges and needn't reach their ends.
There are 2 independent parts, one for each index of `mol`. The reference program is written for one: setup_inputs(seed, part) draws one part's arguments, and reference() takes and returns one part's arrays. A program takes and returns all parts, laid end to end along the dimension named above; an argument that names none is the same for every part. Nothing has to cross between parts.
Inputs may be any that keep to these rules, and one draw needn't show every extreme that they name: `sector_sizes`: at least one sector has exactly 12 blocks; the sizes add up to 128.
All inputs are finite; a program needn't handle non-finite values.
Results may differ from the reference program's by a relative error of at most 0.0001.
Values sent between devices are 32-bit elements; how exact they have to be, the bound alone decides.
A program may use at most 128 MiB of HBM per device.

```python
import math
import jax
import jax.numpy as jnp
import numpy as np
from jax import lax

BLOCK = 128
VB_DEV = 8
SECT_MAX = 12
OPAIRS = 192
NBLK = 128
VPAIRS = 16384
N_VIR = 16


def touch_ends(result, stream_key, smallest, largest):
    longest = result.shape.index(max(result.shape))
    spots = []
    for shift in (0, 1):
        where = [jax.random.randint(jax.random.fold_in(stream_key, axis), (), 0, length) for axis, length in enumerate(result.shape)]
        where[longest] = (where[longest] + shift) % result.shape[longest]
        spots.append(tuple(where))
    return result.at[spots[0]].set(smallest).at[spots[1]].set(largest)


def block_scale(rng, dims, split, low, top_value):
    level, own = 1.0, jax.random.fold_in(rng, 6)
    for position, parts in split:
        draws = jnp.exp(jax.random.uniform(jax.random.fold_in(own, position), (parts,), jnp.float32, low / len(split), top_value / len(split)))
        level = level * jnp.repeat(draws, dims[position] // parts).reshape([-1 if axis == position else 1 for axis in range(len(dims))])
    return level


def split_up(amount, total, most, skew):
    loads = [(1 << 20) // math.isqrt(standing ** skew) + 1 for standing in range(2, amount + 1)]
    surplus, counts = total - most - (amount - 1), [1] * (amount - 1)
    while surplus > 0:
        free = [i for i in range(amount - 1) if counts[i] < most]
        whole, budget = sum([loads[i] for i in free]), surplus
        for i in free:
            addition = min(most - counts[i], max(1, budget * loads[i] // whole), surplus)
            counts[i] = counts[i] + addition
            surplus = surplus - addition
    return np.array([most] + counts)


def ragged_sizes(own_key, number_of, total, limit, slope):
    if number_of == 2:
        one = jax.random.randint(own_key, (), max(1, total - limit), min(limit, total - 1) + 1)
        return jnp.stack([one, total - one])
    sizes = jnp.asarray(split_up(number_of, total, limit, slope), jnp.int32)
    twos = (number_of - 1) // 2
    source_of, receiver = sizes[1:1 + 2 * twos:2], sizes[2:2 + 2 * twos:2]
    margin = jnp.minimum(source_of - 1, limit - receiver)
    shifted = jax.random.randint(jax.random.fold_in(own_key, 1), (twos,), 0, 1 << 20) % (margin + 1)
    sizes = sizes.at[1:1 + 2 * twos:2].set(source_of - shifted).at[2:2 + 2 * twos:2].set(receiver + shifted)
    return sizes[jax.random.permutation(jax.random.fold_in(own_key, 2), number_of)]


def normal_values(rng, extent, deviation, bound, split=(), kind=jnp.bfloat16):
    factor_of = block_scale(rng, extent, split, -0.22, 0.18) if split else 1.0
    result = jax.random.normal(rng, extent, jnp.float32) * deviation * factor_of
    return jnp.minimum(jnp.maximum(result, -bound), bound).astype(kind)


def setup_inputs(seed: int = 0, part: int = 0) -> dict:
    keys = jax.random.split(jax.random.key(seed), 7)
    own_keys = jax.random.split(jax.random.fold_in(keys[6], part), 7)
    amplitudes = normal_values(own_keys[0], (OPAIRS, VPAIRS), 1.0, 6.0, ((1, 16),), jnp.float32)
    ladder_ints = normal_values(own_keys[1], (N_VIR * SECT_MAX * BLOCK, SECT_MAX * BLOCK), (SECT_MAX * BLOCK) ** -0.5, 0.15625, ((0, 16),), jnp.float32)
    hole_ints = normal_values(own_keys[2], (OPAIRS, OPAIRS), OPAIRS ** -0.5, 0.4375, (), jnp.float32)
    sector_sizes = ragged_sizes(keys[3], N_VIR, NBLK, SECT_MAX, 2).astype(jnp.int32)
    device_perm = jax.random.permutation(keys[4], N_VIR).astype(jnp.int32)
    block_shift = touch_ends(jax.random.randint(keys[5], (N_VIR,), 0, VB_DEV), jax.random.fold_in(keys[5], 1), 0, VB_DEV - 1).astype(jnp.int32)
    return {"amplitudes": amplitudes, "ladder_ints": ladder_ints, "hole_ints": hole_ints, "sector_sizes": sector_sizes, "device_perm": device_perm, "block_shift": block_shift}


def select_sum(mask, values):
    return jnp.sum(jnp.where(mask, values[None, :], 0), axis=1).astype(jnp.int32)


def tables(sector_sizes, device_perm, block_shift, vir_count, per_device):
    block_count = per_device * vir_count
    slot_ids = jnp.arange(block_count, dtype=jnp.int32)
    devices = jnp.arange(vir_count, dtype=jnp.int32)
    sector_ends = jnp.cumsum(sector_sizes).astype(jnp.int32)
    sector_starts = (sector_ends - sector_sizes).astype(jnp.int32)
    sector = jnp.sum((sector_ends[None, :] <= slot_ids[:, None]).astype(jnp.int32), axis=1).astype(jnp.int32)
    in_sector = sector[:, None] == devices[None, :]
    sector_rank = (slot_ids - select_sum(in_sector, sector_starts)).astype(jnp.int32)
    column = slot_ids % vir_count
    owner_dev = select_sum(column[:, None] == devices[None, :], device_perm)
    shift_of = select_sum(owner_dev[:, None] == devices[None, :], block_shift)
    local_idx = ((slot_ids // vir_count + shift_of) % per_device).astype(jnp.int32)
    return sector, sector_rank, owner_dev, local_idx


def reference(amplitudes, ladder_ints, hole_ints, sector_sizes, device_perm, block_shift):
    sector, sector_rank, owner_dev, local_idx = tables(sector_sizes, device_perm, block_shift, N_VIR, VB_DEV)
    global_ids = (owner_dev * VB_DEV + local_idx).astype(jnp.int32)
    rank_ids = jnp.arange(SECT_MAX, dtype=jnp.int32)
    sectors = jnp.arange(N_VIR, dtype=jnp.int32)
    hits = (sector[None, None, :] == sectors[:, None, None]) & (sector_rank[None, None, :] == rank_ids[None, :, None])
    members = jnp.sum(jnp.where(hits, global_ids[None, None, :], 0), axis=2).astype(jnp.int32)
    live = rank_ids[None, :] < sector_sizes[:, None]
    rows_all = amplitudes.shape[0]
    blocks = amplitudes.reshape(rows_all, VB_DEV * N_VIR, BLOCK)
    matrices = ladder_ints.reshape(N_VIR, SECT_MAX * BLOCK, SECT_MAX * BLOCK)

    def one_sector(carry, inputs):
        member_ids, alive, matrix = inputs
        picked = jnp.where(alive[None, :, None], jnp.take(blocks, member_ids, axis=1), 0.0)
        product = jnp.dot(picked.reshape(rows_all, SECT_MAX * BLOCK), matrix, precision=lax.Precision.HIGHEST)
        product = jnp.where(alive[None, :, None], product.reshape(rows_all, SECT_MAX, BLOCK), 0.0)
        return carry.at[:, member_ids, :].add(product), None

    particle, unused = lax.scan(one_sector, jnp.zeros_like(blocks), (members, live, matrices))
    hole = jnp.dot(hole_ints, amplitudes, precision=lax.Precision.HIGHEST)
    return particle.reshape(rows_all, VB_DEV * N_VIR * BLOCK) + hole
```

```python
import functools

import jax
import jax.numpy as jnp
from jax import lax
from jax.experimental import pallas as pl
from jax.experimental.pallas import tpu as pltpu
from jax.sharding import PartitionSpec as P

BLOCK = 128
PLANE = 4
CHUNKS = 4
MESH = pl.DeviceIdType.MESH
F32 = jnp.float32
BF16 = jnp.bfloat16


def split(value):
    high = value.astype(BF16)
    return high, (value - high.astype(F32)).astype(BF16)


def loop(count, step, unroll=True):
    def run(index, carry):
        step(index)
        return carry

    lax.fori_loop(0, count, run, 0, unroll=unroll)


def kernel(
    cfg,
    sizes,
    perm,
    shifts,
    amp,
    ladder,
    extra,
    out,
    starts,
    cols,
    tab1,
    tab2,
    tab3,
    tab4,
    tab5,
    tab6,
    raw,
    w_high,
    w_low,
    ladder_sem,
    sems,
    *chunk_refs,
):
    n, per, span, plane, planes, cap, chunks, rows, with_hole = cfg
    rc = rows // chunks
    me = lax.axis_index("vir")
    my_z, my_g = me // plane, me % plane
    bufs = [chunk_refs[k * 10 : (k + 1) * 10] for k in range(chunks)]

    fetch = pltpu.make_async_copy(ladder, raw, ladder_sem)
    fetch.start()

    barrier = pltpu.get_barrier_semaphore()
    z_peers = [((my_z + d) % planes) * plane + my_g for d in range(planes)]
    g_peers = [my_z * plane + (my_g + e) % plane for e in range(plane)]
    peers = z_peers[1:] + g_peers[1:]
    for peer in peers:
        pl.semaphore_signal(barrier, inc=1, device_id={"vir": peer}, device_id_type=MESH)

    def prefix(j, total):
        starts[j] = total
        return total + sizes[j]

    starts[n] = lax.fori_loop(0, n, prefix, jnp.int32(0), unroll=True)

    def find_column(p):
        found = jnp.int32(0)
        for c in range(n):
            found = found + jnp.where(perm[c] == p, c, 0)
        cols[p] = found

    loop(n, find_column, unroll=False)

    def first_slot(start, col):
        return start + (col - start + n * per) % n

    my_col, my_shift = cols[me], shifts[me]
    my_start, my_size = starts[me], sizes[me]
    plane_start = starts[my_z * plane]

    def fill1(q):
        t = first_slot(starts[(q // cap) * plane], my_col) + n * (q % cap)
        tab1[q] = (t // n + my_shift) % per

    loop(planes * cap, fill1)

    def pack1(k):
        s1, r1, own = bufs[k][0], bufs[k][1], bufs[k][9]
        for b in range(per):
            own[b] = amp[k * rc : (k + 1) * rc, b * BLOCK : (b + 1) * BLOCK]
        for d in range(planes):
            z = (my_z + d) % planes
            for i in range(cap):
                block = own[tab1[z * cap + i]]
                if d == 0:
                    r1[my_z * cap + i] = block
                else:
                    s1[d * cap + i] = block

    def z_copy(stage, k, d, src, dst):
        return pltpu.make_async_remote_copy(
            src_ref=src.at[pl.ds(d * cap, cap)],
            dst_ref=dst.at[pl.ds(my_z * cap, cap)],
            send_sem=sems.at[stage, 0, k, d],
            recv_sem=sems.at[stage, 1, k, d],
            device_id={"vir": z_peers[d]},
            device_id_type=MESH,
        )

    def g_copy(stage, k, e, src, dst):
        return pltpu.make_async_remote_copy(
            src_ref=src.at[pl.ds(e * planes, planes)],
            dst_ref=dst.at[pl.ds(my_g * planes, planes)],
            send_sem=sems.at[stage, 0, k, e],
            recv_sem=sems.at[stage, 1, k, e],
            device_id={"vir": g_peers[e]},
            device_id_type=MESH,
        )

    order = sorted(range(1, planes), key=lambda d: abs(d - planes / 2))
    started = []

    def send_z(stage, k, src, dst):
        for d in order:
            copy = z_copy(stage, k, d, src, dst)
            copy.start()
            started.append(copy)

    def send_g(stage, k, src, dst):
        for e in range(1, plane):
            copy = g_copy(stage, k, e, src, dst)
            copy.start()
            started.append(copy)

    def wait_z(stage, k, src, dst):
        for d in range(1, planes):
            z_copy(stage, k, d, src, dst).wait_recv()

    def wait_g(stage, k, src, dst):
        for e in range(1, plane):
            g_copy(stage, k, e, src, dst).wait_recv()

    pack1(0)
    pl.semaphore_wait(barrier, len(peers))
    send_z(0, 0, bufs[0][0], bufs[0][1])
    for k in range(1, chunks):
        pack1(k)
        send_z(0, k, bufs[k][0], bufs[k][1])

    def fill2(q):
        z, j = q // plane, my_z * plane + q % plane
        col = cols[z * plane + my_g]
        t = first_slot(starts[j], col)
        i = (t - first_slot(plane_start, col)) // n
        tab2[q] = z * cap + jnp.minimum(i, cap - 1)

    loop(planes * plane, fill2)

    def fill3(r):
        owner = perm[(my_start + r) % n]
        place = (owner % plane) * planes + owner // plane
        tab3[r] = jnp.where(r < my_size, place, n)

    loop(span, fill3)

    def fill4(q):
        g, z = q // planes, q % planes
        r = (cols[z * plane + g] - my_start + n * per) % n
        tab4[q] = jnp.minimum(r, span - 1)

    loop(planes * plane, fill4)

    def fill5(q):
        z, i = q // cap, q % cap
        t = first_slot(plane_start, cols[z * plane + my_g]) + n * i
        j = jnp.int32(0)
        for step in range(plane - 1):
            j = j + jnp.where(starts[my_z * plane + step + 1] <= t, 1, 0)
        tab5[q] = j * planes + z

    loop(planes * cap, fill5)

    def fill6(b):
        t = ((b + per - my_shift) % per) * n + my_col
        z = jnp.int32(0)
        for step in range(1, planes):
            z = z + jnp.where(starts[step * plane] <= t, 1, 0)
        i = (t - first_slot(starts[z * plane], my_col)) // n
        tab6[b] = z * cap + jnp.minimum(i, cap - 1)

    loop(per, fill6)

    wide = 2 * BLOCK
    if with_hole:
        h_high, h_low = split(extra[...])
        h_both = jnp.concatenate([h_high, h_low], axis=0)

        def hole_tile(c):
            at = pl.ds(pl.multiple_of(c * wide, wide), wide)
            a_high, a_low = split(amp[:, at])
            both = jnp.dot(h_both, a_high, preferred_element_type=F32)
            cross = jnp.dot(h_high, a_low, preferred_element_type=F32)
            out[:, at] = both[:rows] + (both[rows:] + cross)

        loop(per * BLOCK // wide, hole_tile, unroll=False)
    else:
        out[...] = extra[...]

    fetch.wait()
    part = 64

    def split_rows(i):
        at = pl.ds(pl.multiple_of(i * part, part), part)
        high, low = split(raw[at, :])
        w_high[at, :] = high
        w_low[at, :] = low

    loop(span * BLOCK // part, split_rows, unroll=False)

    def stage_a(k):
        s1, r1, s2, r2 = bufs[k][:4]
        wait_z(0, k, s1, r1)
        for e in range(plane):
            j = (my_g + e) % plane
            for z in range(planes):
                block = r1[tab2[z * plane + j]]
                if e == 0:
                    r2[my_g * planes + z] = block
                else:
                    s2[e * planes + z] = block
        send_g(1, k, s2, r2)

    def stage_b(k):
        s2, r2, both, prod, s3, r3 = bufs[k][2:8]
        wait_g(1, k, s2, r2)
        r2[n] = jnp.zeros((rc, BLOCK), F32)
        for r in range(span):
            high, low = split(r2[tab3[r]])
            both[:rc, r * BLOCK : (r + 1) * BLOCK] = high
            both[rc:, r * BLOCK : (r + 1) * BLOCK] = low

        def tile(c):
            at = pl.ds(pl.multiple_of(c * wide, wide), wide)
            main = jnp.dot(both[...], w_high[:, at], preferred_element_type=F32)
            cross = jnp.dot(both[:rc], w_low[:, at], preferred_element_type=F32)
            total = main[:rc] + (main[rc:] + cross)
            for half in range(wide // BLOCK):
                prod[c * (wide // BLOCK) + half] = total[:, half * BLOCK : (half + 1) * BLOCK]

        loop(span * BLOCK // wide, tile, unroll=False)
        for e in range(plane):
            g = (my_g + e) % plane
            for z in range(planes):
                block = prod[tab4[g * planes + z]]
                if e == 0:
                    r3[my_g * planes + z] = block
                else:
                    s3[e * planes + z] = block
        send_g(2, k, s3, r3)

    def stage_c(k):
        s3, r3, r4 = bufs[k][6:9]
        s4 = bufs[k][0]
        wait_g(2, k, s3, r3)
        for d in order:
            z_copy(0, k, d, bufs[k][0], bufs[k][1]).wait_send()
        for d in range(planes):
            z = (my_z + d) % planes
            for i in range(cap):
                block = r3[tab5[z * cap + i]]
                if d == 0:
                    r4[my_z * cap + i] = block
                else:
                    s4[d * cap + i] = block
        send_z(3, k, s4, r4)

    def stage_d(k):
        r4 = bufs[k][8]
        wait_z(3, k, bufs[k][0], r4)
        for b in range(per):
            block = r4[tab6[b]]
            at = (slice(k * rc, (k + 1) * rc), slice(b * BLOCK, (b + 1) * BLOCK))
            out[at] = out[at] + block

    for step in range(chunks + 2):
        if step < chunks:
            stage_a(step)
        if 0 <= step - 1 < chunks:
            stage_b(step - 1)
        if 0 <= step - 2 < chunks:
            stage_c(step - 2)
    for k in range(chunks):
        stage_d(k)
    for k in range(chunks):
        for e in range(1, plane):
            g_copy(1, k, e, bufs[k][2], bufs[k][3]).wait_send()
            g_copy(2, k, e, bufs[k][6], bufs[k][7]).wait_send()
        for d in order:
            z_copy(3, k, d, bufs[k][0], bufs[k][8]).wait_send()


def ladder_call(amplitudes, ladder_ints, extra, sizes, perm, shifts, with_hole):
    n = lax.axis_size("vir")
    rows, width = amplitudes.shape
    per, span = width // BLOCK, ladder_ints.shape[0] // BLOCK
    plane = PLANE if n % PLANE == 0 else 1
    planes = n // plane
    cap = min(per, -(-plane * span // n))
    chunks = CHUNKS if rows % (16 * CHUNKS) == 0 else 1
    rc = rows // chunks
    cfg = (n, per, span, plane, planes, cap, chunks, rows, with_hole)
    blocks = lambda count: pltpu.VMEM((count, rc, BLOCK), F32)
    chunk_scratch = [
        blocks(planes * cap),
        blocks(planes * cap),
        blocks(n),
        blocks(n + 1),
        pltpu.VMEM((2 * rc, span * BLOCK), BF16),
        blocks(span),
        blocks(n),
        blocks(n),
        blocks(planes * cap),
        blocks(per),
    ]
    smem = pl.BlockSpec(memory_space=pltpu.SMEM)
    vmem = pl.BlockSpec(memory_space=pltpu.VMEM)
    table = lambda count: pltpu.SMEM((count,), jnp.int32)
    return pl.pallas_call(
        functools.partial(kernel, cfg),
        out_shape=jax.ShapeDtypeStruct((rows, width), F32),
        in_specs=[smem, smem, smem, vmem, pl.BlockSpec(memory_space=pl.ANY), vmem],
        out_specs=vmem,
        scratch_shapes=[
            table(n + 1),
            table(n),
            table(planes * cap),
            table(n),
            table(span),
            table(n),
            table(planes * cap),
            table(per),
            pltpu.VMEM(ladder_ints.shape, F32),
            pltpu.VMEM(ladder_ints.shape, BF16),
            pltpu.VMEM(ladder_ints.shape, BF16),
            pltpu.SemaphoreType.DMA,
            pltpu.SemaphoreType.DMA((4, 2, chunks, max(plane, planes))),
            *(chunk_scratch * chunks),
        ],
        compiler_params=pltpu.CompilerParams(
            collective_id=0, has_side_effects=True, vmem_limit_bytes=52 * 2**20
        ),
        cost_estimate=pl.CostEstimate(
            flops=6 * rows * (span * BLOCK) ** 2,
            bytes_accessed=4 * (span * BLOCK) ** 2,
            transcendentals=0,
        ),
    )(sizes, perm, shifts, amplitudes, ladder_ints, extra)


def body(amplitudes, ladder_ints, hole_ints, sector_sizes, device_perm, block_shift):
    with_hole = lax.axis_size("occ") == 1
    if with_hole:
        extra = hole_ints
    else:
        partial_sum = jnp.dot(hole_ints, amplitudes, precision=lax.Precision.HIGHEST)
        extra = lax.psum_scatter(partial_sum, "occ", scatter_dimension=0, tiled=True)
    return ladder_call(
        amplitudes, ladder_ints, extra, sector_sizes, device_perm, block_shift, with_hole
    )


def solution(mesh):
    in_specs = (P(("mol", "occ"), "vir"), P(("mol", "vir"), None), P("mol", "occ"), P(), P(), P())
    out_specs = P(("mol", "occ"), "vir")
    return jax.shard_map(body, mesh=mesh, in_specs=in_specs, out_specs=out_specs, check_vma=False)
```

```python
import functools

import jax
import jax.numpy as jnp
from jax import lax
from jax.experimental import pallas as pl
from jax.experimental.pallas import tpu as pltpu
from jax.sharding import PartitionSpec as P

BLOCK = 128
PLANE = 4
CHUNKS = 4
AHEAD = 1
CAP = 3
ORDER = "abc"
MESH = pl.DeviceIdType.MESH
F32 = jnp.float32
BF16 = jnp.bfloat16


def split(value):
    high = value.astype(BF16)
    return high, (value - high.astype(F32)).astype(BF16)


def loop(count, step, unroll=True):
    def run(index, carry):
        step(index)
        return carry

    lax.fori_loop(0, count, run, 0, unroll=unroll)


def kernel(
    cfg,
    sizes_hbm,
    perm_hbm,
    shifts_hbm,
    amp_hbm,
    ladder,
    extra_hbm,
    out,
    sizes,
    perm,
    shifts,
    amp,
    extra,
    starts,
    cols,
    tab1,
    tab2,
    tab3,
    tab4,
    tab5,
    tab6,
    raw,
    w_high,
    w_low,
    load_sems,
    sems,
    *chunk_refs,
):
    n, per, span, plane, planes, cap, chunks, rows, with_hole = cfg
    rc = rows // chunks
    me = lax.axis_index("vir")
    my_z, my_g = me // plane, me % plane
    bufs = [chunk_refs[k * 10 : (k + 1) * 10] for k in range(chunks)]

    barrier = pltpu.get_barrier_semaphore()
    z_peers = [((my_z + d) % planes) * plane + my_g for d in range(planes)]
    g_peers = [my_z * plane + (my_g + e) % plane for e in range(plane)]
    peers = z_peers[1:] + g_peers[1:]
    for peer in peers:
        pl.semaphore_signal(barrier, inc=1, device_id={"vir": peer}, device_id_type=MESH)

    pairs = [
        (sizes_hbm, sizes),
        (perm_hbm, perm),
        (shifts_hbm, shifts),
        (amp_hbm, amp),
        (extra_hbm, extra),
        (ladder, raw),
    ]
    loads = [
        pltpu.make_async_copy(src, dst, load_sems.at[i]) for i, (src, dst) in enumerate(pairs)
    ]
    for load in loads:
        load.start()
    for load in loads[:3]:
        load.wait()

    def prefix(j, total):
        starts[j] = total
        return total + sizes[j]

    starts[n] = lax.fori_loop(0, n, prefix, jnp.int32(0), unroll=True)

    def column_of(p):
        found = jnp.int32(0)
        for c in range(n):
            found = found + jnp.where(perm[c] == p, c, 0)
        return found

    def find_column(p):
        cols[p] = column_of(p)

    def first_slot(start, col):
        return start + (col - start + n * per) % n

    my_col, my_shift = column_of(me), shifts[me]
    my_start, my_size = starts[me], sizes[me]
    plane_start = starts[my_z * plane]

    def fill1(q):
        t = first_slot(starts[(q // cap) * plane], my_col) + n * (q % cap)
        tab1[q] = (t // n + my_shift) % per

    loop(planes * cap, fill1)

    def pack1(k):
        s1, r1, own = bufs[k][0], bufs[k][1], bufs[k][9]
        for b in range(per):
            own[b] = amp[k * rc : (k + 1) * rc, b * BLOCK : (b + 1) * BLOCK]
        for d in range(planes):
            z = (my_z + d) % planes
            for i in range(cap):
                block = own[tab1[z * cap + i]]
                if d == 0:
                    r1[my_z * cap + i] = block
                else:
                    s1[d * cap + i] = block

    def z_copy(stage, k, d, src, dst):
        return pltpu.make_async_remote_copy(
            src_ref=src.at[pl.ds(d * cap, cap)],
            dst_ref=dst.at[pl.ds(my_z * cap, cap)],
            send_sem=sems.at[stage, 0, k, d],
            recv_sem=sems.at[stage, 1, k, d],
            device_id={"vir": z_peers[d]},
            device_id_type=MESH,
        )

    def g_copy(stage, k, e, src, dst):
        return pltpu.make_async_remote_copy(
            src_ref=src.at[pl.ds(e * planes, planes)],
            dst_ref=dst.at[pl.ds(my_g * planes, planes)],
            send_sem=sems.at[stage, 0, k, e],
            recv_sem=sems.at[stage, 1, k, e],
            device_id={"vir": g_peers[e]},
            device_id_type=MESH,
        )

    order = sorted(range(1, planes), key=lambda d: abs(d - planes / 2))

    def send_z(stage, k, src, dst):
        for d in order:
            z_copy(stage, k, d, src, dst).start()

    def send_g(stage, k, src, dst):
        for e in range(1, plane):
            g_copy(stage, k, e, src, dst).start()

    def wait_z(stage, k, src, dst):
        for d in range(1, planes):
            z_copy(stage, k, d, src, dst).wait_recv()

    def wait_g(stage, k, src, dst):
        for e in range(1, plane):
            g_copy(stage, k, e, src, dst).wait_recv()

    loads[3].wait()
    pack1(0)
    pl.semaphore_wait(barrier, len(peers))
    send_z(0, 0, bufs[0][0], bufs[0][1])
    for k in range(1, chunks):
        pack1(k)
        if k < AHEAD:
            send_z(0, k, bufs[k][0], bufs[k][1])

    loop(n, find_column, unroll=False)

    def fill2(q):
        z, j = q // plane, my_z * plane + q % plane
        col = cols[z * plane + my_g]
        t = first_slot(starts[j], col)
        i = (t - first_slot(plane_start, col)) // n
        tab2[q] = z * cap + jnp.minimum(i, cap - 1)

    loop(planes * plane, fill2)

    def fill3(r):
        owner = perm[(my_start + r) % n]
        place = (owner % plane) * planes + owner // plane
        tab3[r] = jnp.where(r < my_size, place, n)

    loop(span, fill3)

    def fill4(q):
        g, z = q // planes, q % planes
        r = (cols[z * plane + g] - my_start + n * per) % n
        tab4[q] = jnp.minimum(r, span - 1)

    loop(planes * plane, fill4)

    def fill5(q):
        z, i = q // cap, q % cap
        t = first_slot(plane_start, cols[z * plane + my_g]) + n * i
        j = jnp.int32(0)
        for step in range(plane - 1):
            j = j + jnp.where(starts[my_z * plane + step + 1] <= t, 1, 0)
        tab5[q] = j * planes + z

    loop(planes * cap, fill5)

    def fill6(b):
        t = ((b + per - my_shift) % per) * n + my_col
        z = jnp.int32(0)
        for step in range(1, planes):
            z = z + jnp.where(starts[step * plane] <= t, 1, 0)
        i = (t - first_slot(starts[z * plane], my_col)) // n
        tab6[b] = z * cap + jnp.minimum(i, cap - 1)

    loop(per, fill6)

    wide = 2 * BLOCK
    loads[4].wait()
    if with_hole:
        h_high, h_low = split(extra[...])
        h_both = jnp.concatenate([h_high, h_low], axis=0)

        def hole_tile(c):
            at = pl.ds(pl.multiple_of(c * wide, wide), wide)
            a_high, a_low = split(amp[:, at])
            both = jnp.dot(h_both, a_high, preferred_element_type=F32)
            cross = jnp.dot(h_high, a_low, preferred_element_type=F32)
            out[:, at] = both[:rows] + (both[rows:] + cross)

        loop(per * BLOCK // wide, hole_tile, unroll=False)
    else:
        out[...] = extra[...]

    loads[5].wait()
    part = 64

    def split_rows(i):
        at = pl.ds(pl.multiple_of(i * part, part), part)
        high, low = split(raw[at, :])
        w_high[at, :] = high
        w_low[at, :] = low

    loop(span * BLOCK // part, split_rows, unroll=False)

    def stage_a(k):
        s1, r1, s2, r2 = bufs[k][:4]
        wait_z(0, k, s1, r1)
        for e in range(plane):
            j = (my_g + e) % plane
            for z in range(planes):
                block = r1[tab2[z * plane + j]]
                if e == 0:
                    r2[my_g * planes + z] = block
                else:
                    s2[e * planes + z] = block
        send_g(1, k, s2, r2)

    def stage_b(k):
        s2, r2, both, prod, s3, r3 = bufs[k][2:8]
        wait_g(1, k, s2, r2)
        r2[n] = jnp.zeros((rc, BLOCK), F32)
        for r in range(span):
            high, low = split(r2[tab3[r]])
            both[:rc, r * BLOCK : (r + 1) * BLOCK] = high
            both[rc:, r * BLOCK : (r + 1) * BLOCK] = low

        def tile(c):
            at = pl.ds(pl.multiple_of(c * wide, wide), wide)
            main = jnp.dot(both[...], w_high[:, at], preferred_element_type=F32)
            cross = jnp.dot(both[:rc], w_low[:, at], preferred_element_type=F32)
            total = main[:rc] + (main[rc:] + cross)
            for half in range(wide // BLOCK):
                prod[c * (wide // BLOCK) + half] = total[:, half * BLOCK : (half + 1) * BLOCK]

        loop(span * BLOCK // wide, tile, unroll=False)
        for e in range(plane):
            g = (my_g + e) % plane
            for z in range(planes):
                block = prod[tab4[g * planes + z]]
                if e == 0:
                    r3[my_g * planes + z] = block
                else:
                    s3[e * planes + z] = block
        send_g(2, k, s3, r3)

    def stage_c(k):
        s3, r3, r4 = bufs[k][6:9]
        s4 = bufs[k][0]
        wait_g(2, k, s3, r3)
        for d in order:
            z_copy(0, k, d, bufs[k][0], bufs[k][1]).wait_send()
        for d in range(planes):
            z = (my_z + d) % planes
            for i in range(cap):
                block = r3[tab5[z * cap + i]]
                if d == 0:
                    r4[my_z * cap + i] = block
                else:
                    s4[d * cap + i] = block
        send_z(3, k, s4, r4)

    def stage_d(k):
        r4 = bufs[k][8]
        wait_z(3, k, bufs[k][0], r4)
        for b in range(per):
            block = r4[tab6[b]]
            at = (slice(k * rc, (k + 1) * rc), slice(b * BLOCK, (b + 1) * BLOCK))
            out[at] = out[at] + block

    stages = {"a": (0, stage_a), "b": (1, stage_b), "c": (2, stage_c)}
    for step in range(chunks + 2):
        for name in ORDER:
            late, stage = stages[name]
            if 0 <= step - late < chunks:
                stage(step - late)
            if name == "a" and AHEAD <= step + AHEAD < chunks:
                send_z(0, step + AHEAD, bufs[step + AHEAD][0], bufs[step + AHEAD][1])
    for k in range(chunks):
        stage_d(k)
    for k in range(chunks):
        for e in range(1, plane):
            g_copy(1, k, e, bufs[k][2], bufs[k][3]).wait_send()
            g_copy(2, k, e, bufs[k][6], bufs[k][7]).wait_send()
        for d in order:
            z_copy(3, k, d, bufs[k][0], bufs[k][8]).wait_send()


def ladder_call(amplitudes, ladder_ints, extra, sizes, perm, shifts, with_hole):
    n = lax.axis_size("vir")
    rows, width = amplitudes.shape
    per, span = width // BLOCK, ladder_ints.shape[0] // BLOCK
    plane = PLANE if n % PLANE == 0 else 1
    planes = n // plane
    cap = min(CAP, per, -(-plane * span // n))
    chunks = CHUNKS if rows % (16 * CHUNKS) == 0 else 1
    rc = rows // chunks
    cfg = (n, per, span, plane, planes, cap, chunks, rows, with_hole)
    blocks = lambda count: pltpu.VMEM((count, rc, BLOCK), F32)
    chunk_scratch = [
        blocks(planes * cap),
        blocks(planes * cap),
        blocks(n),
        blocks(n + 1),
        pltpu.VMEM((2 * rc, span * BLOCK), BF16),
        blocks(span),
        blocks(n),
        blocks(n),
        blocks(planes * cap),
        blocks(per),
    ]
    table = lambda count: pltpu.SMEM((count,), jnp.int32)
    return pl.pallas_call(
        functools.partial(kernel, cfg),
        out_shape=jax.ShapeDtypeStruct((rows, width), F32),
        in_specs=[pl.BlockSpec(memory_space=pl.ANY)] * 6,
        out_specs=pl.BlockSpec(memory_space=pltpu.VMEM),
        scratch_shapes=[
            table(n),
            table(n),
            table(n),
            pltpu.VMEM((rows, width), F32),
            pltpu.VMEM(extra.shape, F32),
            table(n + 1),
            table(n),
            table(planes * cap),
            table(n),
            table(span),
            table(n),
            table(planes * cap),
            table(per),
            pltpu.VMEM(ladder_ints.shape, F32),
            pltpu.VMEM(ladder_ints.shape, BF16),
            pltpu.VMEM(ladder_ints.shape, BF16),
            pltpu.SemaphoreType.DMA((6,)),
            pltpu.SemaphoreType.DMA((4, 2, chunks, max(plane, planes))),
            *(chunk_scratch * chunks),
        ],
        compiler_params=pltpu.CompilerParams(
            collective_id=0, has_side_effects=True, vmem_limit_bytes=60 * 2**20
        ),
        cost_estimate=pl.CostEstimate(
            flops=6 * rows * (span * BLOCK) ** 2,
            bytes_accessed=4 * (span * BLOCK) ** 2,
            transcendentals=0,
        ),
    )(sizes, perm, shifts, amplitudes, ladder_ints, extra)


def body(amplitudes, ladder_ints, hole_ints, sector_sizes, device_perm, block_shift):
    with_hole = lax.axis_size("occ") == 1
    if with_hole:
        extra = hole_ints
    else:
        partial_sum = jnp.dot(hole_ints, amplitudes, precision=lax.Precision.HIGHEST)
        extra = lax.psum_scatter(partial_sum, "occ", scatter_dimension=0, tiled=True)
    return ladder_call(
        amplitudes, ladder_ints, extra, sector_sizes, device_perm, block_shift, with_hole
    )


def solution(mesh):
    in_specs = (P(("mol", "occ"), "vir"), P(("mol", "vir"), None), P("mol", "occ"), P(), P(), P())
    out_specs = P(("mol", "occ"), "vir")
    return jax.shard_map(body, mesh=mesh, in_specs=in_specs, out_specs=out_specs, check_vma=False)
```

```python
import functools

import jax
import jax.numpy as jnp
from jax import lax
from jax.experimental import pallas as pl
from jax.experimental.pallas import tpu as pltpu
from jax.sharding import PartitionSpec as P

BLOCK = 128
PLANE = 4
CHUNKS = 4
AHEAD = 1
CAP = 3
ORDER = "abc"
MESH = pl.DeviceIdType.MESH
F32 = jnp.float32
BF16 = jnp.bfloat16


def split(value):
    high = value.astype(BF16)
    return high, (value - high.astype(F32)).astype(BF16)


def loop(count, step, unroll=True):
    def run(index, carry):
        step(index)
        return carry

    lax.fori_loop(0, count, run, 0, unroll=unroll)


def kernel(
    cfg,
    sizes_hbm,
    perm_hbm,
    shifts_hbm,
    amp_hbm,
    ladder,
    extra_hbm,
    out,
    sizes,
    perm,
    shifts,
    amp,
    extra,
    starts,
    cols,
    tab1,
    tab2,
    tab3,
    tab4,
    tab5,
    tab6,
    raw,
    w_high,
    w_low,
    load_sems,
    sems,
    *chunk_refs,
):
    n, per, span, plane, planes, cap, chunks, rows, with_hole = cfg
    rc = rows // chunks
    me = lax.axis_index("vir")
    my_z, my_g = me // plane, me % plane
    bufs = [chunk_refs[k * 10 : (k + 1) * 10] for k in range(chunks)]

    barrier = pltpu.get_barrier_semaphore()
    z_peers = [((my_z + d) % planes) * plane + my_g for d in range(planes)]
    g_peers = [my_z * plane + (my_g + e) % plane for e in range(plane)]
    peers = z_peers[1:] + g_peers[1:]
    for peer in peers:
        pl.semaphore_signal(barrier, inc=1, device_id={"vir": peer}, device_id_type=MESH)

    pairs = [
        (sizes_hbm, sizes),
        (perm_hbm, perm),
        (shifts_hbm, shifts),
    ]
    for k in range(chunks):
        part = pl.ds(k * rc, rc)
        pairs.append((amp_hbm.at[part], amp.at[part]))
    pairs += [(extra_hbm, extra), (ladder, raw)]
    loads = [
        pltpu.make_async_copy(src, dst, load_sems.at[i]) for i, (src, dst) in enumerate(pairs)
    ]
    for load in loads:
        load.start()
    for load in loads[:3]:
        load.wait()

    def prefix(j, total):
        starts[j] = total
        return total + sizes[j]

    starts[n] = lax.fori_loop(0, n, prefix, jnp.int32(0), unroll=True)

    def column_of(p):
        found = jnp.int32(0)
        for c in range(n):
            found = found + jnp.where(perm[c] == p, c, 0)
        return found

    def find_column(p):
        cols[p] = column_of(p)

    def first_slot(start, col):
        return start + (col - start + n * per) % n

    my_col, my_shift = column_of(me), shifts[me]
    my_start, my_size = starts[me], sizes[me]
    plane_start = starts[my_z * plane]

    def fill1(q):
        t = first_slot(starts[(q // cap) * plane], my_col) + n * (q % cap)
        tab1[q] = (t // n + my_shift) % per

    loop(planes * cap, fill1)

    def pack1(k):
        s1, r1, own = bufs[k][0], bufs[k][1], bufs[k][9]
        for b in range(per):
            own[b] = amp[k * rc : (k + 1) * rc, b * BLOCK : (b + 1) * BLOCK]
        for d in range(planes):
            z = (my_z + d) % planes
            for i in range(cap):
                block = own[tab1[z * cap + i]]
                if d == 0:
                    r1[my_z * cap + i] = block
                else:
                    s1[d * cap + i] = block

    def z_copy(stage, k, d, src, dst):
        return pltpu.make_async_remote_copy(
            src_ref=src.at[pl.ds(d * cap, cap)],
            dst_ref=dst.at[pl.ds(my_z * cap, cap)],
            send_sem=sems.at[stage, 0, k, d],
            recv_sem=sems.at[stage, 1, k, d],
            device_id={"vir": z_peers[d]},
            device_id_type=MESH,
        )

    def g_copy(stage, k, e, src, dst):
        return pltpu.make_async_remote_copy(
            src_ref=src.at[pl.ds(e * planes, planes)],
            dst_ref=dst.at[pl.ds(my_g * planes, planes)],
            send_sem=sems.at[stage, 0, k, e],
            recv_sem=sems.at[stage, 1, k, e],
            device_id={"vir": g_peers[e]},
            device_id_type=MESH,
        )

    order = sorted(range(1, planes), key=lambda d: abs(d - planes / 2))

    def send_z(stage, k, src, dst):
        for d in order:
            z_copy(stage, k, d, src, dst).start()

    def send_g(stage, k, src, dst):
        for e in range(1, plane):
            g_copy(stage, k, e, src, dst).start()

    def wait_z(stage, k, src, dst):
        for d in range(1, planes):
            z_copy(stage, k, d, src, dst).wait_recv()

    def wait_g(stage, k, src, dst):
        for e in range(1, plane):
            g_copy(stage, k, e, src, dst).wait_recv()

    loads[3].wait()
    pack1(0)
    pl.semaphore_wait(barrier, len(peers))
    send_z(0, 0, bufs[0][0], bufs[0][1])
    for k in range(1, chunks):
        loads[3 + k].wait()
        pack1(k)
        if k < AHEAD:
            send_z(0, k, bufs[k][0], bufs[k][1])

    loop(n, find_column, unroll=False)

    def fill2(q):
        z, j = q // plane, my_z * plane + q % plane
        col = cols[z * plane + my_g]
        t = first_slot(starts[j], col)
        i = (t - first_slot(plane_start, col)) // n
        tab2[q] = z * cap + jnp.minimum(i, cap - 1)

    loop(planes * plane, fill2)

    def fill3(r):
        owner = perm[(my_start + r) % n]
        place = (owner % plane) * planes + owner // plane
        tab3[r] = jnp.where(r < my_size, place, n)

    loop(span, fill3)

    def fill4(q):
        g, z = q // planes, q % planes
        r = (cols[z * plane + g] - my_start + n * per) % n
        tab4[q] = jnp.minimum(r, span - 1)

    loop(planes * plane, fill4)

    def fill5(q):
        z, i = q // cap, q % cap
        t = first_slot(plane_start, cols[z * plane + my_g]) + n * i
        j = jnp.int32(0)
        for step in range(plane - 1):
            j = j + jnp.where(starts[my_z * plane + step + 1] <= t, 1, 0)
        tab5[q] = j * planes + z

    loop(planes * cap, fill5)

    def fill6(b):
        t = ((b + per - my_shift) % per) * n + my_col
        z = jnp.int32(0)
        for step in range(1, planes):
            z = z + jnp.where(starts[step * plane] <= t, 1, 0)
        i = (t - first_slot(starts[z * plane], my_col)) // n
        tab6[b] = z * cap + jnp.minimum(i, cap - 1)

    loop(per, fill6)

    wide = 2 * BLOCK
    loads[3 + chunks].wait()
    if with_hole:
        h_high, h_low = split(extra[...])
        h_both = jnp.concatenate([h_high, h_low], axis=0)

        def hole_tile(c):
            at = pl.ds(pl.multiple_of(c * wide, wide), wide)
            a_high, a_low = split(amp[:, at])
            both = jnp.dot(h_both, a_high, preferred_element_type=F32)
            cross = jnp.dot(h_high, a_low, preferred_element_type=F32)
            out[:, at] = both[:rows] + (both[rows:] + cross)

        loop(per * BLOCK // wide, hole_tile, unroll=False)
    else:
        out[...] = extra[...]

    loads[4 + chunks].wait()
    part = 64

    def split_rows(i):
        at = pl.ds(pl.multiple_of(i * part, part), part)
        high, low = split(raw[at, :])
        w_high[at, :] = high
        w_low[at, :] = low

    loop(span * BLOCK // part, split_rows, unroll=False)

    def stage_a(k):
        s1, r1, s2, r2 = bufs[k][:4]
        wait_z(0, k, s1, r1)
        for e in range(plane):
            j = (my_g + e) % plane
            for z in range(planes):
                block = r1[tab2[z * plane + j]]
                if e == 0:
                    r2[my_g * planes + z] = block
                else:
                    s2[e * planes + z] = block
        send_g(1, k, s2, r2)

    def stage_b(k):
        s2, r2, both, prod, s3, r3 = bufs[k][2:8]
        wait_g(1, k, s2, r2)
        r2[n] = jnp.zeros((rc, BLOCK), F32)
        for r in range(span):
            high, low = split(r2[tab3[r]])
            both[:rc, r * BLOCK : (r + 1) * BLOCK] = high
            both[rc:, r * BLOCK : (r + 1) * BLOCK] = low

        def tile(c):
            at = pl.ds(pl.multiple_of(c * wide, wide), wide)
            main = jnp.dot(both[...], w_high[:, at], preferred_element_type=F32)
            cross = jnp.dot(both[:rc], w_low[:, at], preferred_element_type=F32)
            total = main[:rc] + (main[rc:] + cross)
            for half in range(wide // BLOCK):
                prod[c * (wide // BLOCK) + half] = total[:, half * BLOCK : (half + 1) * BLOCK]

        loop(span * BLOCK // wide, tile, unroll=False)
        for e in range(plane):
            g = (my_g + e) % plane
            for z in range(planes):
                block = prod[tab4[g * planes + z]]
                if e == 0:
                    r3[my_g * planes + z] = block
                else:
                    s3[e * planes + z] = block
        send_g(2, k, s3, r3)

    def stage_c(k):
        s3, r3, r4 = bufs[k][6:9]
        s4 = bufs[k][0]
        wait_g(2, k, s3, r3)
        for d in order:
            z_copy(0, k, d, bufs[k][0], bufs[k][1]).wait_send()
        for d in range(planes):
            z = (my_z + d) % planes
            for i in range(cap):
                block = r3[tab5[z * cap + i]]
                if d == 0:
                    r4[my_z * cap + i] = block
                else:
                    s4[d * cap + i] = block
        send_z(3, k, s4, r4)

    def stage_d(k):
        r4 = bufs[k][8]
        wait_z(3, k, bufs[k][0], r4)
        for b in range(per):
            block = r4[tab6[b]]
            at = (slice(k * rc, (k + 1) * rc), slice(b * BLOCK, (b + 1) * BLOCK))
            out[at] = out[at] + block

    stages = {"a": (0, stage_a), "b": (1, stage_b), "c": (2, stage_c)}
    for step in range(chunks + 2):
        for name in ORDER:
            late, stage = stages[name]
            if 0 <= step - late < chunks:
                stage(step - late)
            if name == "a" and AHEAD <= step + AHEAD < chunks:
                send_z(0, step + AHEAD, bufs[step + AHEAD][0], bufs[step + AHEAD][1])
    for k in range(chunks):
        stage_d(k)
    for k in range(chunks):
        for e in range(1, plane):
            g_copy(1, k, e, bufs[k][2], bufs[k][3]).wait_send()
            g_copy(2, k, e, bufs[k][6], bufs[k][7]).wait_send()
        for d in order:
            z_copy(3, k, d, bufs[k][0], bufs[k][8]).wait_send()


def ladder_call(amplitudes, ladder_ints, extra, sizes, perm, shifts, with_hole):
    n = lax.axis_size("vir")
    rows, width = amplitudes.shape
    per, span = width // BLOCK, ladder_ints.shape[0] // BLOCK
    plane = PLANE if n % PLANE == 0 else 1
    planes = n // plane
    cap = min(CAP, per, -(-plane * span // n))
    chunks = CHUNKS if rows % (16 * CHUNKS) == 0 else 1
    rc = rows // chunks
    cfg = (n, per, span, plane, planes, cap, chunks, rows, with_hole)
    blocks = lambda count: pltpu.VMEM((count, rc, BLOCK), F32)
    chunk_scratch = [
        blocks(planes * cap),
        blocks(planes * cap),
        blocks(n),
        blocks(n + 1),
        pltpu.VMEM((2 * rc, span * BLOCK), BF16),
        blocks(span),
        blocks(n),
        blocks(n),
        blocks(planes * cap),
        blocks(per),
    ]
    table = lambda count: pltpu.SMEM((count,), jnp.int32)
    return pl.pallas_call(
        functools.partial(kernel, cfg),
        out_shape=jax.ShapeDtypeStruct((rows, width), F32),
        in_specs=[pl.BlockSpec(memory_space=pl.ANY)] * 6,
        out_specs=pl.BlockSpec(memory_space=pltpu.VMEM),
        scratch_shapes=[
            table(n),
            table(n),
            table(n),
            pltpu.VMEM((rows, width), F32),
            pltpu.VMEM(extra.shape, F32),
            table(n + 1),
            table(n),
            table(planes * cap),
            table(n),
            table(span),
            table(n),
            table(planes * cap),
            table(per),
            pltpu.VMEM(ladder_ints.shape, F32),
            pltpu.VMEM(ladder_ints.shape, BF16),
            pltpu.VMEM(ladder_ints.shape, BF16),
            pltpu.SemaphoreType.DMA((5 + chunks,)),
            pltpu.SemaphoreType.DMA((4, 2, chunks, max(plane, planes))),
            *(chunk_scratch * chunks),
        ],
        compiler_params=pltpu.CompilerParams(
            collective_id=0, has_side_effects=True, vmem_limit_bytes=60 * 2**20
        ),
        cost_estimate=pl.CostEstimate(
            flops=6 * rows * (span * BLOCK) ** 2,
            bytes_accessed=4 * (span * BLOCK) ** 2,
            transcendentals=0,
        ),
    )(sizes, perm, shifts, amplitudes, ladder_ints, extra)


def body(amplitudes, ladder_ints, hole_ints, sector_sizes, device_perm, block_shift):
    with_hole = lax.axis_size("occ") == 1
    if with_hole:
        extra = hole_ints
    else:
        partial_sum = jnp.dot(hole_ints, amplitudes, precision=lax.Precision.HIGHEST)
        extra = lax.psum_scatter(partial_sum, "occ", scatter_dimension=0, tiled=True)
    return ladder_call(
        amplitudes, ladder_ints, extra, sector_sizes, device_perm, block_shift, with_hole
    )


def solution(mesh):
    in_specs = (P(("mol", "occ"), "vir"), P(("mol", "vir"), None), P("mol", "occ"), P(), P(), P())
    out_specs = P(("mol", "occ"), "vir")
    return jax.shard_map(body, mesh=mesh, in_specs=in_specs, out_specs=out_specs, check_vma=False)
```
